256 devices in a mesh: qb: 16 (over z, core), kb: 16 (over y, x).
Axes of the slice: x: 4, y: 4, z: 8, core: 2. Of those that a mesh axis runs over, the one named last changes fastest.
Arguments:
- queries: float32 [16384, 1024], P(('qb', 'kb')), may hold values from -300 to 300
- keys: float32 [16384, 128], P(('qb', 'kb')), may hold values from -7 to 7, as said below
- values: float32 [16384, 128], P(('qb', 'kb')), may hold values from -6 to 6
- block_mask: int32 [512, 512], replicated, may hold values 0 or 1
- key_lengths: int32 [16384], replicated, may hold values from 1 to 16384, as said below
Outputs:
- attended: float32 [16384, 1024], P(('qb', 'kb'))
- log_norm: float32 [8, 16384], P(None, ('qb', 'kb'))
The draws below stay inside these ranges and needn't reach their ends.
Inputs may be any that keep to these rules, and one draw needn't show every extreme that they name: keys are of order one. key_lengths[r] lies between min(r + 1, 64) and r + 1; the last row has 16384.
All inputs are finite; a program needn't handle non-finite values.
Results may differ from the reference program's by a relative error of at most 0.0003.
Values sent between devices are 32-bit elements; how exact they have to be, the bound alone decides.
A program may use at most 64 MiB of HBM per device.

```python
import jax
import jax.numpy as jnp
from jax import lax

HEADS = 8
HEAD_DIM = 128
MBLK = 32
TOKENS = 16384
NBLK = 512


def paired_keys(key):
    base = jnp.clip(jax.random.normal(jax.random.fold_in(key, 101), (TOKENS, HEAD_DIM), jnp.float32), -6.0, 6.0)
    return base


def draw_keys(key, part):
    return paired_keys(key)


def draw_queries(key, part):
    key = jax.random.fold_in(key, 7)
    drawn = jnp.clip(jax.random.normal(key, (TOKENS, HEADS * HEAD_DIM), jnp.float32), -6.0, 6.0)
    return drawn


def draw_key_lengths(key, part):
    key = jax.random.fold_in(key, 3)
    extra = jax.random.randint(key, (TOKENS,), 0, TOKENS)
    index = jnp.arange(TOKENS, dtype=jnp.int32)
    lengths = jnp.minimum(index + 1, 64 + extra)
    return jnp.where(index == TOKENS - 1, TOKENS, lengths).astype(jnp.int32)


def with_ends(drawn, stream_key, smallest, largest):
    longest = drawn.shape.index(max(drawn.shape))
    spots = []
    for shift in (0, 1):
        where = [jax.random.randint(jax.random.fold_in(stream_key, axis), (), 0, length) for axis, length in enumerate(drawn.shape)]
        where[longest] = (where[longest] + shift) % drawn.shape[longest]
        spots.append(tuple(where))
    return drawn.at[spots[0]].set(smallest).at[spots[1]].set(largest)


def levels(key, dims, split, low, largest):
    loudness, own = 1.0, jax.random.fold_in(key, 6)
    for position, shards_of in split:
        heights = jnp.exp(jax.random.uniform(jax.random.fold_in(own, position), (shards_of,), jnp.float32, low / len(split), largest / len(split)))
        loudness = loudness * jnp.repeat(heights, dims[position] // shards_of).reshape([-1 if axis == position else 1 for axis in range(len(dims))])
    return loudness


def normal_values(rng, extent, scale, limit, pieces=(), kind=jnp.bfloat16):
    factor_of = levels(rng, extent, pieces, -0.22, 0.18) if pieces else 1.0
    entries = jax.random.normal(rng, extent, jnp.float32) * scale * factor_of
    return jnp.minimum(jnp.maximum(entries, -limit), limit).astype(kind)


def setup_inputs(seed: int = 0) -> dict:
    key_of = jax.random.split(jax.random.key(seed), 6)
    return {
        "queries": draw_queries(jax.random.fold_in(key_of[5], 71), 0),
        "keys": draw_keys(jax.random.fold_in(key_of[5], 71), 0),
        "values": normal_values(key_of[2], (TOKENS, HEAD_DIM), 1.0, 6.0, ((0, 256),), jnp.float32),
        "block_mask": with_ends((jax.random.randint(key_of[3], (NBLK, NBLK), 0, 4) < 3).astype(jnp.int32), jax.random.fold_in(key_of[3], 1), 0, 1),
        "key_lengths": draw_key_lengths(jax.random.fold_in(key_of[5], 71), 0),
    }


NEG = -1.0e30


def reference(queries, keys, values, block_mask, key_lengths):
    rblk = 256
    nblocks = TOKENS // rblk
    scale = 1.0 / (HEAD_DIM ** 0.5)
    key_pos = jnp.arange(TOKENS, dtype=jnp.int32)

    def one_block(index):
        start = (index * rblk).astype(jnp.int32)
        rows_q = lax.dynamic_slice_in_dim(queries, start, rblk, 0).reshape(rblk, HEADS, HEAD_DIM)
        row_pos = start + jnp.arange(rblk, dtype=jnp.int32)
        lengths = lax.dynamic_slice_in_dim(key_lengths, start, rblk, 0)
        mask_rows = lax.dynamic_slice_in_dim(block_mask, (start // MBLK).astype(jnp.int32), rblk // MBLK, 0)
        coarse = jnp.repeat(jnp.repeat(mask_rows, MBLK, axis=0), MBLK, axis=1)
        diff = row_pos[:, None] - key_pos[None, :]
        same = (row_pos[:, None] // MBLK) == (key_pos[None, :] // MBLK)
        allowed = (diff >= 0) & (diff < lengths[:, None]) & ((coarse == 1) | same)
        score = jnp.einsum("rhd,cd->hrc", rows_q, keys, precision=lax.Precision.HIGHEST) * scale
        masked = jnp.where(allowed[None], score, NEG)
        row_max = jnp.max(masked, axis=2)
        weight = jnp.where(allowed[None], jnp.exp(masked - row_max[:, :, None]), 0.0)
        total = jnp.sum(weight, axis=2)
        out = jnp.einsum("hrc,cd->rhd", weight, values, precision=lax.Precision.HIGHEST)
        out = out / jnp.transpose(total)[:, :, None]
        return out.reshape(rblk, HEADS * HEAD_DIM), row_max + jnp.log(total)

    outs, norms = lax.map(one_block, jnp.arange(nblocks, dtype=jnp.int32))
    attended = outs.reshape(TOKENS, HEADS * HEAD_DIM)
    log_norm = jnp.transpose(norms, (1, 0, 2)).reshape(HEADS, TOKENS)
    return attended, log_norm
```

```python
import functools
import math

import jax
import jax.numpy as jnp
from jax import lax
from jax.experimental import pallas as pl
from jax.experimental.pallas import tpu as pltpu
from jax.sharding import PartitionSpec as P

HEADS = 8
HEAD_DIM = 128
TOK = 64
PAIRS = HEADS * TOK
NX, NY, NZ = 4, 4, 8
TILE = 2 * NY * TOK
NEG = -1e30
FLOOR = -1e29
BIG = 1 << 30
MESH = pl.DeviceIdType.MESH
F32 = jnp.float32
BF16 = jnp.bfloat16
KT = 256


def split(x):
    hi = x.astype(BF16)
    lo = (x - hi.astype(F32)).astype(BF16)
    return hi, lo


def kernel(
    q_ref, k_ref, v_ref, bm_ref, kl_ref, out_ref, ln_ref,
    qbuf, qcat, kvbuf, kcat, vcat, s, mx, acc, lacc, osend, lsend, orecv, lrecv, own, bm, lens, cp,
    local_sem, qs, qr, zs, zr, ys, yr, cs, cr, os_, or_, ls_, lr_,
):
    qb = lax.axis_index("qb")
    kb = lax.axis_index("kb")
    z, c = lax.div(qb, 2), lax.rem(qb, 2)
    y, x = lax.div(kb, NX), lax.rem(kb, NX)
    gr = qb * NY + y
    partner = (qb + 1 - 2 * c, kb)

    def at_x(d):
        return (qb, y * NX + lax.rem(x + d, NX))

    def at_y(d):
        return (qb, lax.rem(y + d, NY) * NX + x)

    def at_z(d):
        return (lax.rem(qb + 2 * d, 2 * NZ), kb)

    loads = [
        pltpu.make_async_copy(k_ref, kvbuf.at[0, z, c, y], local_sem.at[0]),
        pltpu.make_async_copy(v_ref, kvbuf.at[1, z, c, y], local_sem.at[1]),
        pltpu.make_async_copy(q_ref, qbuf.at[x], local_sem.at[2]),
        pltpu.make_async_copy(bm_ref.at[pl.ds(pl.multiple_of(gr * 8, 8), 8)], bm, local_sem.at[3]),
        pltpu.make_async_copy(kl_ref.at[pl.ds(pl.multiple_of(qb * 8, 8), 8)], lens, local_sem.at[4]),
    ]
    for copy in loads:
        copy.start()

    barrier = pltpu.get_barrier_semaphore()
    peers = [at_x(d) for d in (1, 2, 3)] + [at_y(d) for d in (1, 2, 3)] + [at_z(d) for d in range(1, NZ)] + [partner]
    for peer in peers:
        pl.semaphore_signal(barrier, inc=1, device_id=peer, device_id_type=MESH)
    for copy in loads:
        copy.wait()
    pl.semaphore_wait(barrier, len(peers))

    def q_copy(d):
        return pltpu.make_async_remote_copy(
            src_ref=qbuf.at[x], dst_ref=qbuf.at[x], send_sem=qs.at[d], recv_sem=qr.at[x],
            device_id=at_x(d), device_id_type=MESH)

    def q_arrival(d):
        src = lax.rem(x + d, NX)
        return pltpu.make_async_remote_copy(
            src_ref=qbuf.at[src], dst_ref=qbuf.at[src], send_sem=qs.at[0], recv_sem=qr.at[src],
            device_id=at_x(d), device_id_type=MESH)

    def z_copy(w, d):
        return pltpu.make_async_remote_copy(
            src_ref=kvbuf.at[w, z, c, y], dst_ref=kvbuf.at[w, z, c, y], send_sem=zs.at[w, d], recv_sem=zr.at[w, z],
            device_id=at_z(d), device_id_type=MESH)

    def z_arrival(w, zz):
        return pltpu.make_async_remote_copy(
            src_ref=kvbuf.at[w, zz, c, y], dst_ref=kvbuf.at[w, zz, c, y], send_sem=zs.at[w, 0], recv_sem=zr.at[w, zz],
            device_id=at_z(1), device_id_type=MESH)

    def y_copy(w, zz, d):
        return pltpu.make_async_remote_copy(
            src_ref=kvbuf.at[w, zz, c, y], dst_ref=kvbuf.at[w, zz, c, y], send_sem=ys.at[w, zz, d], recv_sem=yr.at[w, zz, y],
            device_id=at_y(d), device_id_type=MESH)

    def y_arrival(w, zz, d):
        src = lax.rem(y + d, NY)
        return pltpu.make_async_remote_copy(
            src_ref=kvbuf.at[w, zz, c, src], dst_ref=kvbuf.at[w, zz, c, src], send_sem=ys.at[w, zz, 0],
            recv_sem=yr.at[w, zz, src], device_id=at_y(d), device_id_type=MESH)

    def c_copy(w, zz):
        return pltpu.make_async_remote_copy(
            src_ref=kvbuf.at[w, zz, c], dst_ref=kvbuf.at[w, zz, c], send_sem=cs.at[w, zz], recv_sem=cr.at[w, zz],
            device_id=partner, device_id_type=MESH)

    def c_arrival(w, zz):
        return pltpu.make_async_remote_copy(
            src_ref=kvbuf.at[w, zz, 1 - c], dst_ref=kvbuf.at[w, zz, 1 - c], send_sem=cs.at[w, zz], recv_sem=cr.at[w, zz],
            device_id=partner, device_id_type=MESH)

    def o_copy(d):
        return pltpu.make_async_remote_copy(
            src_ref=osend.at[d - 1], dst_ref=orecv.at[d - 1], send_sem=os_.at[d], recv_sem=or_.at[d],
            device_id=at_x(d), device_id_type=MESH)

    def l_copy(d):
        return pltpu.make_async_remote_copy(
            src_ref=lsend.at[d - 1], dst_ref=lrecv.at[d - 1], send_sem=ls_.at[d], recv_sem=lr_.at[d],
            device_id=at_x(d), device_id_type=MESH)

    def stage_a(w, i):
        zz = z - i

        @pl.when(i > 0)
        def _():
            z_arrival(w, zz).wait_recv()
        for d in (1, 3, 2):
            y_copy(w, zz, d).start()

    def stage_b(w, i):
        zz = z - i
        for d in (1, 3, 2):
            y_arrival(w, zz, d).wait_recv()
        c_copy(w, zz).start()

    stage_a(0, 0)
    for d in (1, 3):
        q_copy(d).start()

    def send_z(w):
        def step(d, carry):
            z_copy(w, d).start()
            return carry
        lax.fori_loop(1, NZ - z, step, 0)

    send_z(0)
    q_copy(2).start()
    send_z(1)

    lane = lax.broadcasted_iota(jnp.int32, (8, 128), 1)
    sub = lax.broadcasted_iota(jnp.int32, (8, 128), 0)
    pick = 8 * (lane // 64) + 2 * x + (lane // 32) % 2
    for n in range(NZ * TILE // 128):
        bits = bm[:, (n // 8) * 128:(n // 8 + 1) * 128]
        here = jnp.take_along_axis(bits, pick + 16 * (n % 8), axis=1)
        column = 16 * n + pick
        token = 256 * (2 * n + lane // 64) + 64 * x + lane % 64
        cp[:, n * 128:(n + 1) * 128] = jnp.where((here == 1) | (column == 8 * gr + sub), token, BIG)

    scale = math.log2(math.e) / math.sqrt(HEAD_DIM)
    lane64 = lax.broadcasted_iota(jnp.int32, (TOK, 128), 1)
    sub64 = lax.broadcasted_iota(jnp.int32, (TOK, 128), 0)
    eye = lane64 == sub64

    def prepare_q(j):
        for h in range(HEADS):
            hi, lo = split(qbuf[j, :, h * HEAD_DIM:(h + 1) * HEAD_DIM] * scale)
            for i, part in enumerate((hi, lo, hi, lo)):
                qcat[j, h * TOK:(h + 1) * TOK, i * 128:(i + 1) * 128] = part
        mx[j] = jnp.full((PAIRS, 128), NEG, F32)

    def prepare_k(zz):
        hi, lo = split(kvbuf[0, zz].reshape(TILE, HEAD_DIM))
        rows = pl.ds(pl.multiple_of(zz * TILE, TILE), TILE)
        for i, part in enumerate((hi, hi, lo, lo)):
            kcat[rows, i * 128:(i + 1) * 128] = part

    def prepare_v(zz):
        hi, lo = split(kvbuf[1, zz].reshape(TILE, HEAD_DIM))
        rows = pl.ds(pl.multiple_of(zz * TILE, TILE), TILE)
        vcat[rows, :128] = hi
        vcat[rows, 128:] = lo

    def scores(j, zz):
        length_row = lens[pl.ds(2 * y + j // 2, 1), :]
        length = jnp.max(
            jnp.where(lane64 == sub64 + 64 * (j % 2), jnp.broadcast_to(length_row, (TOK, 128)), 0), axis=1, keepdims=True)
        row = 256 * gr + 64 * j + lax.broadcasted_iota(jnp.int32, (TOK, KT), 0)
        low = row - length
        for n in range(TILE // KT):
            off = pl.multiple_of(zz * TILE + n * KT, KT)
            sc = lax.dot_general(
                qcat[j], kcat[pl.ds(off, KT), :], (((1,), (1,)), ((), ())), preferred_element_type=F32)
            tokens = jnp.concatenate(
                [jnp.broadcast_to(cp[pl.ds(2 * j + i, 1), pl.ds(off, KT)], (32, KT)) for i in range(2)], axis=0)
            ok = (tokens <= row) & (tokens > low)
            sc = jnp.where(ok[None], sc.reshape(HEADS, TOK, KT), NEG).reshape(PAIRS, KT)
            s[j, :, pl.ds(off, KT)] = sc
            m = mx[j]
            for a in range(KT // 128):
                m = jnp.maximum(m, sc[:, a * 128:(a + 1) * 128])
            mx[j] = m

    prepare_q(x)

    stage_b(0, 0)

    @pl.when(z >= 1)
    def _():
        stage_a(0, 1)

    def own_step(i, carry):
        @pl.when(i + 2 <= z)
        def _():
            stage_a(0, i + 2)

        @pl.when(i + 1 <= z)
        def _():
            stage_b(0, i + 1)
        c_arrival(0, z - i).wait_recv()
        prepare_k(z - i)
        scores(x, z - i)
        return carry

    lax.fori_loop(0, z + 1, own_step, 0)

    for turn, d in enumerate((1, 3, 2)):
        q_arrival(d).wait_recv()
        j = lax.rem(x + d, NX)
        prepare_q(j)

        def other_step(i, carry, turn=turn, j=j):
            if turn == 0:
                stage_a(1, i)
            elif turn == 1:
                stage_b(1, i)
            else:
                c_arrival(1, z - i).wait_recv()
                prepare_v(z - i)
            scores(j, z - i)
            return carry

        lax.fori_loop(0, z + 1, other_step, 0)

    def attend(j, write):
        m = jnp.maximum(jnp.max(mx[j], axis=1, keepdims=True), FLOOR)
        mx[j] = jnp.broadcast_to(m, (PAIRS, 128))
        acc[...] = jnp.zeros_like(acc)
        lacc[...] = jnp.zeros_like(lacc)

        def part(off, width):
            shift = jnp.concatenate([mx[j]] * (width // 128), axis=1)
            p = jnp.exp2(s[j, :, pl.ds(off, width)] - shift)
            hi, lo = split(p)
            v = vcat[pl.ds(off, width), :]
            acc[...] += jnp.dot(hi, v, preferred_element_type=F32) + jnp.dot(lo, v, preferred_element_type=F32)
            total = p[:, :128]
            for a in range(1, width // 128):
                total = total + p[:, a * 128:(a + 1) * 128]
            lacc[...] += total

        def pair_step(i, carry):
            part(pl.multiple_of(i * 2 * TILE, 2 * TILE), 2 * TILE)
            return carry

        lax.fori_loop(0, (z + 1) // 2, pair_step, 0)

        @pl.when(z % 2 == 0)
        def _():
            part(pl.multiple_of(z * TILE, TILE), TILE)

        total = jnp.sum(lacc[...], axis=1, keepdims=True)
        some = total > 0
        inverse = jnp.where(some, 1.0 / jnp.where(some, total, 1.0), 0.0)
        lse = jnp.where(some, m + jnp.log2(jnp.where(some, total, 1.0)), NEG)
        write((acc[:, :128] + acc[:, 128:]) * inverse, lse)

    def to_lanes(lse):
        spread = jnp.broadcast_to(lse, (PAIRS, 128)).reshape(HEADS, TOK, 128)
        return jnp.sum(jnp.where(eye[None], spread, 0.0), axis=1)

    for d in (1, 3, 2):
        def write(value, lse, d=d):
            osend[d - 1] = value
            lsend[d - 1] = to_lanes(lse)
            o_copy(d).start()
            l_copy(d).start()
        attend(lax.rem(x + d, NX), write)

    def write_own(value, lse):
        own[...] = value
        lsend[3] = to_lanes(lse)
    attend(x, write_own)

    for d in (1, 3, 2):
        o_copy(d).wait_recv()
        l_copy(d).wait_recv()
    parts = [lsend[3], lrecv[0], lrecv[1], lrecv[2]]
    top = functools.reduce(jnp.maximum, parts)
    weights = [jnp.exp2(part - top) for part in parts]
    total = weights[0] + weights[1] + weights[2] + weights[3]
    ln_ref[...] = ((top + jnp.log2(total)) * math.log(2.0))[:, :TOK]
    shares = [weight / total for weight in weights]
    for h in range(HEADS):
        rows = slice(h * TOK, (h + 1) * TOK)
        blocks = [own[rows, :], orecv[0, rows, :], orecv[1, rows, :], orecv[2, rows, :]]
        result = jnp.zeros((TOK, 128), F32)
        for share, block in zip(shares, blocks):
            column = jnp.sum(jnp.where(eye, jnp.broadcast_to(share[h:h + 1, :], (TOK, 128)), 0.0), axis=1, keepdims=True)
            result = result + column * block
        out_ref[:, h * HEAD_DIM:(h + 1) * HEAD_DIM] = result

    for d in (1, 2, 3):
        q_copy(d).wait_send()
        o_copy(d).wait_send()
        l_copy(d).wait_send()

    def drain_z(d, carry):
        z_copy(0, d).wait_send()
        z_copy(1, d).wait_send()
        return carry

    lax.fori_loop(1, NZ - z, drain_z, 0)

    def drain(i, carry):
        for w in range(2):
            for d in (1, 2, 3):
                y_copy(w, z - i, d).wait_send()
            c_copy(w, z - i).wait_send()
        return carry

    lax.fori_loop(0, z + 1, drain, 0)


def shards(queries, keys, values, block_mask, key_lengths):
    lengths = key_lengths.reshape(128, 128)
    dma = pltpu.SemaphoreType.DMA
    anywhere = pl.BlockSpec(memory_space=pl.ANY)
    vmem = pl.BlockSpec(memory_space=pltpu.VMEM)
    return pl.pallas_call(
        kernel,
        out_shape=(
            jax.ShapeDtypeStruct((TOK, HEADS * HEAD_DIM), F32),
            jax.ShapeDtypeStruct((HEADS, TOK), F32),
        ),
        in_specs=[anywhere] * 5,
        out_specs=(vmem, vmem),
        scratch_shapes=[
            pltpu.VMEM((NX, TOK, HEADS * HEAD_DIM), F32),
            pltpu.VMEM((NX, PAIRS, 512), BF16),
            pltpu.VMEM((2, NZ, 2, NY, TOK, HEAD_DIM), F32),
            pltpu.VMEM((NZ * TILE, 512), BF16),
            pltpu.VMEM((NZ * TILE, 256), BF16),
            pltpu.VMEM((NX, PAIRS, NZ * TILE), F32),
            pltpu.VMEM((NX, PAIRS, 128), F32),
            pltpu.VMEM((PAIRS, 256), F32),
            pltpu.VMEM((PAIRS, 128), F32),
            pltpu.VMEM((3, PAIRS, 128), F32),
            pltpu.VMEM((4, HEADS, 128), F32),
            pltpu.VMEM((3, PAIRS, 128), F32),
            pltpu.VMEM((3, HEADS, 128), F32),
            pltpu.VMEM((PAIRS, 128), F32),
            pltpu.VMEM((8, 512), jnp.int32),
            pltpu.VMEM((8, 128), jnp.int32),
            pltpu.VMEM((8, NZ * TILE), jnp.int32),
            dma((5,)),
            dma((NX,)), dma((NX,)),
            dma((2, NZ)), dma((2, NZ)),
            dma((2, NZ, NY)), dma((2, NZ, NY)),
            dma((2, NZ)), dma((2, NZ)),
            dma((4,)), dma((4,)), dma((4,)), dma((4,)),
        ],
        compiler_params=pltpu.CompilerParams(
            vmem_limit_bytes=60 * 2**20, collective_id=0, has_side_effects=True),
        cost_estimate=pl.CostEstimate(flops=8 * 2 * 128 * 2**22, bytes_accessed=2**22, transcendentals=2**22),
    )(queries, keys, values, block_mask, lengths)


def solution(mesh):
    in_specs = (P(("qb", "kb"), None), P(("qb", "kb"), None), P(("qb", "kb"), None), P(), P())
    out_specs = (P(("qb", "kb"), None), P(None, ("qb", "kb")))
    return jax.shard_map(shards, mesh=mesh, in_specs=in_specs, out_specs=out_specs, check_vma=False)
```

```python
import functools
import math

import jax
import jax.numpy as jnp
from jax import lax
from jax.experimental import pallas as pl
from jax.experimental.pallas import tpu as pltpu
from jax.sharding import PartitionSpec as P

HEADS = 8
HEAD_DIM = 128
TOK = 64
PAIRS = HEADS * TOK
NX, NY, NZ = 4, 4, 8
TILE = 2 * NY * TOK
NEG = -1e30
FLOOR = -1e29
BIG = 1 << 30
MESH = pl.DeviceIdType.MESH
F32 = jnp.float32
BF16 = jnp.bfloat16
STEP = 2 * TILE
DELTAS = (0, 1, 3, 2)
AHEAD_A, AHEAD_B, AHEAD_C = 10, 6, 2


def split(x):
    hi = x.astype(BF16)
    lo = (x - hi.astype(F32)).astype(BF16)
    return hi, lo


def kernel(
    q_ref, k_ref, v_ref, bm_ref, kl_ref, out_ref, ln_ref,
    qbuf, qcat, kvbuf, kcat, vcat, s, mx, acc, lacc, osend, lsend, orecv, lrecv, own, bm, lens, low, cp,
    local_sem, qs, qr, zs, zr, ys, yr, hs, hr, cs, cr, os_, or_, ls_, lr_,
):
    qb = lax.axis_index("qb")
    kb = lax.axis_index("kb")
    z, c = lax.div(qb, 2), lax.rem(qb, 2)
    y, x = lax.div(kb, NX), lax.rem(kb, NX)
    gr = qb * NY + y
    last = 2 * z + 1
    partner = (qb + 1 - 2 * c, kb)

    def at_x(d):
        return (qb, y * NX + lax.rem(x + d, NX))

    def at_y(d):
        return (qb, lax.rem(y + d, NY) * NX + x)

    def at_z(d):
        return (lax.rem(qb + 2 * d, 2 * NZ), kb)

    loads = [
        pltpu.make_async_copy(k_ref, kvbuf.at[0, z, c, y], local_sem.at[0]),
        pltpu.make_async_copy(v_ref, kvbuf.at[1, z, c, y], local_sem.at[1]),
        pltpu.make_async_copy(q_ref, qbuf.at[x], local_sem.at[2]),
        pltpu.make_async_copy(bm_ref.at[pl.ds(pl.multiple_of(gr * 8, 8), 8)], bm, local_sem.at[3]),
        pltpu.make_async_copy(kl_ref.at[pl.ds(pl.multiple_of(qb * 8, 8), 8)], lens, local_sem.at[4]),
    ]
    for copy in loads:
        copy.start()

    barrier = pltpu.get_barrier_semaphore()
    peers = [at_x(d) for d in (1, 2, 3)] + [at_y(d) for d in (1, 3)] + [at_z(d) for d in range(1, NZ)] + [partner]
    for peer in peers:
        pl.semaphore_signal(barrier, inc=1, device_id=peer, device_id_type=MESH)
    for copy in loads:
        copy.wait()
    pl.semaphore_wait(barrier, len(peers))

    def remote(ref, send_sem, recv_sem, device, dst=None):
        return pltpu.make_async_remote_copy(
            src_ref=ref, dst_ref=ref if dst is None else dst, send_sem=send_sem, recv_sem=recv_sem,
            device_id=device, device_id_type=MESH)

    def q_copy(d):
        return remote(qbuf.at[x], qs.at[d], qr.at[x], at_x(d))

    def q_arrival(d):
        src = lax.rem(x + d, NX)
        return remote(qbuf.at[src], qs.at[0], qr.at[src], at_x(d))

    def z_copy(w, d):
        return remote(kvbuf.at[w, z, c, y], zs.at[w, d], zr.at[w, z], at_z(d))

    def z_arrival(w, zz):
        return remote(kvbuf.at[w, zz, c, y], zs.at[w, 0], zr.at[w, zz], at_z(1))

    def y_copy(w, zz, d):
        return remote(kvbuf.at[w, zz, c, y], ys.at[w, zz, d], yr.at[w, zz, y], at_y(d))

    def y_arrival(w, zz, d):
        src = lax.rem(y + d, NY)
        return remote(kvbuf.at[w, zz, c, src], ys.at[w, zz, 0], yr.at[w, zz, src], at_y(d))

    def half_copy(w, zz, n):
        src = lax.rem(y + (3, 1)[n], NY)
        return remote(kvbuf.at[w, zz, c, src, pl.ds(n * 32, 32)], hs.at[w, zz, n], hr.at[w, zz, n], at_y((1, 3)[n]))

    def half_arrival(w, zz, n):
        src = lax.rem(y + 2, NY)
        return remote(kvbuf.at[w, zz, c, src, pl.ds(n * 32, 32)], hs.at[w, zz, n], hr.at[w, zz, n], at_y(1))

    def c_copy(w, zz):
        return remote(kvbuf.at[w, zz, c], cs.at[w, zz], cr.at[w, zz], partner)

    def c_arrival(w, zz):
        return remote(kvbuf.at[w, zz, 1 - c], cs.at[w, zz], cr.at[w, zz], partner)

    def o_copy(d):
        return remote(osend.at[d - 1], os_.at[d], or_.at[d], at_x(d), orecv.at[d - 1])

    def l_copy(d):
        return remote(lsend.at[d - 1], ls_.at[d], lr_.at[d], at_x(d), lrecv.at[d - 1])

    def place(u):
        w = (u > z).astype(jnp.int32)
        return w, z - u + w * (z + 1)

    def stage_a(u):
        w, zz = place(u)

        @pl.when(zz != z)
        def _():
            z_arrival(w, zz).wait_recv()
        for d in (1, 3):
            y_copy(w, zz, d).start()

    def stage_b(u):
        w, zz = place(u)
        for n, d in ((0, 3), (1, 1)):
            y_arrival(w, zz, d).wait_recv()
            half_copy(w, zz, n).start()

    def stage_c(u):
        w, zz = place(u)
        for n in range(2):
            half_arrival(w, zz, n).wait_recv()
        c_copy(w, zz).start()

    def advance(u):
        for stage, ahead in ((stage_c, AHEAD_C), (stage_b, AHEAD_B), (stage_a, AHEAD_A)):
            step = u + ahead

            @pl.when((step >= 0) & (step <= last))
            def _(stage=stage, step=step):
                stage(step)

    stage_a(0)
    for d in (1, 3):
        q_copy(d).start()

    def send_z(w):
        def step(d, carry):
            z_copy(w, d).start()
            return carry
        lax.fori_loop(1, NZ - z, step, 0)

    send_z(0)
    q_copy(2).start()
    send_z(1)

    lane = lax.broadcasted_iota(jnp.int32, (8, 128), 1)
    sub = lax.broadcasted_iota(jnp.int32, (8, 128), 0)
    pick = 8 * (lane // 64) + 2 * x + (lane // 32) % 2
    for n in range(NZ * TILE // 128):
        bits = bm[:, (n // 8) * 128:(n // 8 + 1) * 128]
        here = jnp.take_along_axis(bits, pick + 16 * (n % 8), axis=1)
        column = 16 * n + pick
        token = 256 * (2 * n + lane // 64) + 64 * x + lane % 64
        cp[:, n * 128:(n + 1) * 128] = jnp.where((here == 1) | (column == 8 * gr + sub), token, BIG)

    scale = math.log2(math.e) / math.sqrt(HEAD_DIM)
    lane64 = lax.broadcasted_iota(jnp.int32, (TOK, 128), 1)
    sub64 = lax.broadcasted_iota(jnp.int32, (TOK, 128), 0)
    eye = lane64 == sub64

    def block_of(slot):
        return lax.rem(x + DELTAS[slot], NX)

    for slot in range(NX):
        j = block_of(slot)
        length_row = lens[pl.ds(2 * y + j // 2, 1), :]
        length = jnp.max(
            jnp.where(lane64 == sub64 + 64 * (j % 2), jnp.broadcast_to(length_row, (TOK, 128)), 0), axis=1, keepdims=True)
        low[slot] = 256 * gr + 64 * j + sub64 - length

    mx[...] = jnp.full(mx.shape, NEG, F32)

    def prepare_q(slot):
        j = block_of(slot)
        for h in range(HEADS):
            rows = slice(slot * PAIRS + h * TOK, slot * PAIRS + (h + 1) * TOK)
            hi, lo = split(qbuf[j, :, h * HEAD_DIM:(h + 1) * HEAD_DIM] * scale)
            for i, part in enumerate((hi, lo, hi, lo)):
                qcat[rows, i * 128:(i + 1) * 128] = part

    def prepare_k(zz):
        hi, lo = split(kvbuf[0, zz].reshape(TILE, HEAD_DIM))
        rows = pl.ds(pl.multiple_of(zz * TILE, TILE), TILE)
        for i, part in enumerate((hi, hi, lo, lo)):
            kcat[rows, i * 128:(i + 1) * 128] = part

    def prepare_v(zz):
        hi, lo = split(kvbuf[1, zz].reshape(TILE, HEAD_DIM))
        rows = pl.ds(pl.multiple_of(zz * TILE, TILE), TILE)
        vcat[rows, :128] = hi
        vcat[rows, 128:] = lo

    def scores(first, count, zz):
        keys = pl.ds(pl.multiple_of(zz * TILE, TILE), TILE)
        raw = lax.dot_general(
            qcat[first * PAIRS:(first + count) * PAIRS, :], kcat[keys, :], (((1,), (1,)), ((), ())),
            preferred_element_type=F32)
        for n in range(count):
            slot = first + n
            j = block_of(slot)
            rows = slice(slot * PAIRS, (slot + 1) * PAIRS)
            tokens = jnp.concatenate(
                [jnp.broadcast_to(cp[pl.ds(2 * j + i, 1), keys], (32, TILE)) for i in range(2)], axis=0)
            row = 256 * gr + 64 * j + lax.broadcasted_iota(jnp.int32, (TOK, TILE), 0)
            ok = (tokens <= row) & (tokens > jnp.concatenate([low[slot]] * (TILE // 128), axis=1))
            sc = raw[n * PAIRS:(n + 1) * PAIRS].reshape(HEADS, TOK, TILE)
            sc = jnp.where(ok[None], sc, NEG).reshape(PAIRS, TILE)
            s[rows, keys] = sc
            m = mx[rows, :]
            for a in range(TILE // 128):
                m = jnp.maximum(m, sc[:, a * 128:(a + 1) * 128])
            mx[rows, :] = m

    prepare_q(0)

    def warm(u, carry):
        advance(u)
        return carry

    lax.fori_loop(1 - AHEAD_A, 0, warm, 0)
    planes = z + 1

    for slot in (1, 2):
        q_arrival(DELTAS[slot]).wait_recv()
        prepare_q(slot)

    def near_step(u, carry):
        advance(u)
        c_arrival(0, z - u).wait_recv()
        prepare_k(z - u)
        scores(1, 2, z - u)
        return carry

    lax.fori_loop(0, planes, near_step, 0)

    q_arrival(DELTAS[3]).wait_recv()
    prepare_q(3)

    def slot_rows(slot):
        return pl.ds(pl.multiple_of(slot * PAIRS, PAIRS), PAIRS)

    def settle_max(slot, carry):
        rows = slot_rows(slot)
        m = jnp.maximum(jnp.max(mx[rows, :], axis=1, keepdims=True), FLOOR)
        mx[rows, :] = jnp.broadcast_to(m, (PAIRS, 128))
        return carry

    acc[...] = jnp.zeros_like(acc)
    lacc[...] = jnp.zeros_like(lacc)

    def weigh(slot, start, width):
        rows = slot_rows(slot)
        keys = pl.ds(pl.multiple_of(start * TILE, TILE), width)
        shift = jnp.concatenate([mx[rows, :]] * (width // 128), axis=1)
        p = jnp.exp2(s[rows, keys] - shift)
        hi, lo = split(p)
        v = vcat[keys, :]
        acc[rows, :] += jnp.dot(hi, v, preferred_element_type=F32) + jnp.dot(lo, v, preferred_element_type=F32)
        total = p[:, :128]
        for a in range(1, width // 128):
            total = total + p[:, a * 128:(a + 1) * 128]
        lacc[rows, :] += total

    def weigh_pair(slot, g):
        weigh(slot, z - 2 * g - 1, STEP)

    pairs = planes // 2

    early = ((3, 3, 0), (4, 3, 1), (5, 2, 0), (6, 3, 2), (7, 2, 1))

    def value_step(k, carry):
        advance(planes + k)
        for n in range(3):
            @pl.when(3 * k + n < planes)
            def _(n=n):
                scores(3, 1, z - 3 * k - n)

        @pl.when(k == jnp.minimum(z, 2))
        def _():
            lax.fori_loop(1, NX, settle_max, 0)
        @pl.when(k >= 3)
        def _():
            second = (k == 5) | (k == 7)
            weigh_pair(jnp.where(second, 2, 3), jnp.where(k == 6, 2, jnp.where((k == 4) | (k == 7), 1, 0)))
        c_arrival(1, z - k).wait_recv()
        prepare_v(z - k)
        return carry

    lax.fori_loop(0, planes, value_step, 0)

    def to_lanes(lse):
        spread = jnp.broadcast_to(lse, (PAIRS, 128)).reshape(HEADS, TOK, 128)
        return jnp.sum(jnp.where(eye[None], spread, 0.0), axis=1)

    def attend(slot, done):
        def pair_step(g, carry):
            weigh_pair(slot, g)
            return carry

        lax.fori_loop(done, pairs, pair_step, 0)

        @pl.when(planes % 2 == 1)
        def _():
            weigh(slot, 0, TILE)
        rows = slice(slot * PAIRS, (slot + 1) * PAIRS)
        total = jnp.sum(lacc[rows, :], axis=1, keepdims=True)
        some = total > 0
        inverse = jnp.where(some, 1.0 / jnp.where(some, total, 1.0), 0.0)
        lse = jnp.where(some, mx[rows, :] + jnp.log2(jnp.where(some, total, 1.0)), NEG)
        return (acc[rows, :128] + acc[rows, 128:]) * inverse, to_lanes(lse)

    for slot in (3, 2, 1):
        d = DELTAS[slot]
        done = jnp.int32(0)
        for k, of, _ in early:
            if of == slot:
                done += (planes > k).astype(jnp.int32)
        value, lse = attend(slot, done)
        lsend[d - 1] = lse
        l_copy(d).start()
        osend[d - 1] = value
        o_copy(d).start()

    def own_step(u, carry):
        scores(0, 1, z - u)
        return carry

    lax.fori_loop(0, planes, own_step, 0)
    settle_max(0, 0)
    value, lse = attend(0, 0)
    own[...] = value
    lsend[3] = lse

    for d in (1, 3, 2):
        l_copy(d).wait_recv()
    parts = [lsend[3], lrecv[0], lrecv[1], lrecv[2]]
    top = functools.reduce(jnp.maximum, parts)
    weights = [jnp.exp2(part - top) for part in parts]
    total = weights[0] + weights[1] + weights[2] + weights[3]
    ln_ref[...] = ((top + jnp.log2(total)) * math.log(2.0))[:, :TOK]
    shares = [weight / total for weight in weights]

    def column(share, h):
        return jnp.sum(jnp.where(eye, jnp.broadcast_to(share[h:h + 1, :], (TOK, 128)), 0.0), axis=1, keepdims=True)

    for h in range(HEADS):
        rows = slice(h * TOK, (h + 1) * TOK)
        out_ref[:, h * HEAD_DIM:(h + 1) * HEAD_DIM] = own[rows, :] * column(shares[0], h)
    for d in (2, 3, 1):
        o_copy(d).wait_recv()
        for h in range(HEADS):
            rows = slice(h * TOK, (h + 1) * TOK)
            out_ref[:, h * HEAD_DIM:(h + 1) * HEAD_DIM] += orecv[d - 1, rows, :] * column(shares[d], h)

    for d in (1, 2, 3):
        q_copy(d).wait_send()
        o_copy(d).wait_send()
        l_copy(d).wait_send()

    def drain_z(d, carry):
        z_copy(0, d).wait_send()
        z_copy(1, d).wait_send()
        return carry

    lax.fori_loop(1, NZ - z, drain_z, 0)

    def drain(u, carry):
        w, zz = place(u)
        for d in (1, 3):
            y_copy(w, zz, d).wait_send()
        for n in range(2):
            half_copy(w, zz, n).wait_send()
        c_copy(w, zz).wait_send()
        return carry

    lax.fori_loop(0, last + 1, drain, 0)


def shards(queries, keys, values, block_mask, key_lengths):
    lengths = key_lengths.reshape(128, 128)
    dma = pltpu.SemaphoreType.DMA
    anywhere = pl.BlockSpec(memory_space=pl.ANY)
    vmem = pl.BlockSpec(memory_space=pltpu.VMEM)
    return pl.pallas_call(
        kernel,
        out_shape=(
            jax.ShapeDtypeStruct((TOK, HEADS * HEAD_DIM), F32),
            jax.ShapeDtypeStruct((HEADS, TOK), F32),
        ),
        in_specs=[anywhere] * 5,
        out_specs=(vmem, vmem),
        scratch_shapes=[
            pltpu.VMEM((NX, TOK, HEADS * HEAD_DIM), F32),
            pltpu.VMEM((NX * PAIRS, 512), BF16),
            pltpu.VMEM((2, NZ, 2, NY, TOK, HEAD_DIM), F32),
            pltpu.VMEM((NZ * TILE, 512), BF16),
            pltpu.VMEM((NZ * TILE, 256), BF16),
            pltpu.VMEM((NX * PAIRS, NZ * TILE), F32),
            pltpu.VMEM((NX * PAIRS, 128), F32),
            pltpu.VMEM((NX * PAIRS, 256), F32),
            pltpu.VMEM((NX * PAIRS, 128), F32),
            pltpu.VMEM((3, PAIRS, 128), F32),
            pltpu.VMEM((4, HEADS, 128), F32),
            pltpu.VMEM((3, PAIRS, 128), F32),
            pltpu.VMEM((3, HEADS, 128), F32),
            pltpu.VMEM((PAIRS, 128), F32),
            pltpu.VMEM((8, 512), jnp.int32),
            pltpu.VMEM((8, 128), jnp.int32),
            pltpu.VMEM((NX, TOK, 128), jnp.int32),
            pltpu.VMEM((8, NZ * TILE), jnp.int32),
            dma((5,)),
            dma((NX,)), dma((NX,)),
            dma((2, NZ)), dma((2, NZ)),
            dma((2, NZ, NY)), dma((2, NZ, NY)),
            dma((2, NZ, 2)), dma((2, NZ, 2)),
            dma((2, NZ)), dma((2, NZ)),
            dma((4,)), dma((4,)), dma((4,)), dma((4,)),
        ],
        compiler_params=pltpu.CompilerParams(
            vmem_limit_bytes=60 * 2**20, collective_id=0, has_side_effects=True),
        cost_estimate=pl.CostEstimate(flops=8 * 2 * 128 * 2**22, bytes_accessed=2**22, transcendentals=2**22),
    )(queries, keys, values, block_mask, lengths)


def solution(mesh):
    in_specs = (P(("qb", "kb"), None), P(("qb", "kb"), None), P(("qb", "kb"), None), P(), P())
    out_specs = (P(("qb", "kb"), None), P(None, ("qb", "kb")))
    return jax.shard_map(shards, mesh=mesh, in_specs=in_specs, out_specs=out_specs, check_vma=False)
```

```python
import functools
import math

import jax
import jax.numpy as jnp
from jax import lax
from jax.experimental import pallas as pl
from jax.experimental.pallas import tpu as pltpu
from jax.sharding import PartitionSpec as P

HEADS = 8
HEAD_DIM = 128
TOK = 64
PAIRS = HEADS * TOK
NX, NY, NZ = 4, 4, 8
TILE = 2 * NY * TOK
NEG = -1e30
FLOOR = -1e29
BIG = 1 << 30
MESH = pl.DeviceIdType.MESH
F32 = jnp.float32
BF16 = jnp.bfloat16
STEP = 2 * TILE
DELTAS = (0, 1, 3, 2)
AHEAD_A, AHEAD_C = 7, 2


def split(x):
    hi = x.astype(BF16)
    lo = (x - hi.astype(F32)).astype(BF16)
    return hi, lo


def kernel(
    q_ref, k_ref, v_ref, bm_ref, kl_ref, out_ref, ln_ref,
    qbuf, qcat, kvbuf, kcat, vcat, s, mx, acc, lacc, osend, lsend, orecv, lrecv, own, bm, lens, low, cp,
    local_sem, qs, qr, zs, zr, zf, ys, yr, cs, cr, os_, or_, ls_, lr_,
):
    qb = lax.axis_index("qb")
    kb = lax.axis_index("kb")
    z, c = lax.div(qb, 2), lax.rem(qb, 2)
    y, x = lax.div(kb, NX), lax.rem(kb, NX)
    gr = qb * NY + y
    last = 2 * z + 1
    partner = (qb + 1 - 2 * c, kb)

    def at_x(d):
        return (qb, y * NX + lax.rem(x + d, NX))

    def at_y(d):
        return (qb, lax.rem(y + d, NY) * NX + x)

    def at_z(d):
        return (lax.rem(qb + 2 * d, 2 * NZ), kb)

    loads = [
        pltpu.make_async_copy(k_ref, kvbuf.at[0, z, c, y], local_sem.at[0]),
        pltpu.make_async_copy(v_ref, kvbuf.at[1, z, c, y], local_sem.at[1]),
        pltpu.make_async_copy(q_ref, qbuf.at[x], local_sem.at[2]),
        pltpu.make_async_copy(bm_ref.at[pl.ds(pl.multiple_of(gr * 8, 8), 8)], bm, local_sem.at[3]),
        pltpu.make_async_copy(kl_ref.at[pl.ds(pl.multiple_of(qb * 8, 8), 8)], lens, local_sem.at[4]),
    ]
    for copy in loads:
        copy.start()

    barrier = pltpu.get_barrier_semaphore()
    peers = [at_x(d) for d in (1, 2, 3)] + [at_y(d) for d in (1, 2, 3)] + [at_z(d) for d in range(1, NZ)] + [partner]
    for peer in peers:
        pl.semaphore_signal(barrier, inc=1, device_id=peer, device_id_type=MESH)
    for copy in loads:
        copy.wait()
    pl.semaphore_wait(barrier, len(peers))

    def remote(ref, send_sem, recv_sem, device, dst=None):
        return pltpu.make_async_remote_copy(
            src_ref=ref, dst_ref=ref if dst is None else dst, send_sem=send_sem, recv_sem=recv_sem,
            device_id=device, device_id_type=MESH)

    def q_copy(d):
        return remote(qbuf.at[x], qs.at[d], qr.at[x], at_x(d))

    def q_arrival(d):
        src = lax.rem(x + d, NX)
        return remote(qbuf.at[src], qs.at[0], qr.at[src], at_x(d))

    def z_copy(w, d):
        return remote(kvbuf.at[w, z, c, y], zs.at[w, d], zr.at[w, z], at_z(d))

    def straight(d):
        return (d < 3) | (d > 4) | (z + d == NZ - 1)

    def forward(w, e):
        return remote(kvbuf.at[w, z - 2, c, y], zf.at[w, e], zr.at[w, z - 2], at_z(e))

    def z_arrival(w, zz):
        return remote(kvbuf.at[w, zz, c, y], zs.at[w, 0], zr.at[w, zz], at_z(1))

    def y_copy(w, zz, d):
        return remote(kvbuf.at[w, zz, c, y], ys.at[w, zz, d], yr.at[w, zz, y], at_y(d))

    def y_arrival(w, zz, d):
        src = lax.rem(y + d, NY)
        return remote(kvbuf.at[w, zz, c, src], ys.at[w, zz, 0], yr.at[w, zz, src], at_y(d))

    def c_copy(w, zz):
        return remote(kvbuf.at[w, zz, c], cs.at[w, zz], cr.at[w, zz], partner)

    def c_arrival(w, zz):
        return remote(kvbuf.at[w, zz, 1 - c], cs.at[w, zz], cr.at[w, zz], partner)

    def o_copy(d):
        return remote(osend.at[d - 1], os_.at[d], or_.at[d], at_x(d), orecv.at[d - 1])

    def l_copy(d):
        return remote(lsend.at[d - 1], ls_.at[d], lr_.at[d], at_x(d), lrecv.at[d - 1])

    def place(u):
        w = (u > z).astype(jnp.int32)
        return w, z - u + w * (z + 1)

    def stage_a(u):
        w, zz = place(u)

        @pl.when(zz != z)
        def _():
            z_arrival(w, zz).wait_recv()
        for e in (1, 2):
            @pl.when((zz == z - 2) & (z + e < NZ - 1))
            def _(e=e):
                forward(w, e).start()
        for d in (2, 1, 3):
            y_copy(w, zz, d).start()

    def stage_c(u):
        w, zz = place(u)
        for d in (1, 3, 2):
            y_arrival(w, zz, d).wait_recv()
        c_copy(w, zz).start()

    def advance(u):
        for stage, ahead in ((stage_c, AHEAD_C), (stage_a, AHEAD_A)):
            step = u + ahead

            @pl.when((step >= 0) & (step <= last))
            def _(stage=stage, step=step):
                stage(step)

    stage_a(0)
    for d in (1, 3):
        q_copy(d).start()

    def send_z(w):
        def step(d, carry):
            @pl.when(straight(d))
            def _():
                z_copy(w, d).start()
            return carry
        lax.fori_loop(1, NZ - z, step, 0)

    send_z(0)
    q_copy(2).start()
    send_z(1)

    lane = lax.broadcasted_iota(jnp.int32, (8, 128), 1)
    sub = lax.broadcasted_iota(jnp.int32, (8, 128), 0)
    pick = 8 * (lane // 64) + 2 * x + (lane // 32) % 2
    for n in range(NZ * TILE // 128):
        bits = bm[:, (n // 8) * 128:(n // 8 + 1) * 128]
        here = jnp.take_along_axis(bits, pick + 16 * (n % 8), axis=1)
        column = 16 * n + pick
        token = 256 * (2 * n + lane // 64) + 64 * x + lane % 64
        cp[:, n * 128:(n + 1) * 128] = jnp.where((here == 1) | (column == 8 * gr + sub), token, BIG)

    scale = math.log2(math.e) / math.sqrt(HEAD_DIM)
    lane64 = lax.broadcasted_iota(jnp.int32, (TOK, 128), 1)
    sub64 = lax.broadcasted_iota(jnp.int32, (TOK, 128), 0)
    eye = lane64 == sub64

    def block_of(slot):
        return lax.rem(x + DELTAS[slot], NX)

    for slot in range(NX):
        j = block_of(slot)
        length_row = lens[pl.ds(2 * y + j // 2, 1), :]
        length = jnp.max(
            jnp.where(lane64 == sub64 + 64 * (j % 2), jnp.broadcast_to(length_row, (TOK, 128)), 0), axis=1, keepdims=True)
        low[slot] = 256 * gr + 64 * j + sub64 - length

    mx[...] = jnp.full(mx.shape, NEG, F32)

    def prepare_q(slot):
        j = block_of(slot)
        for h in range(HEADS):
            rows = slice(slot * PAIRS + h * TOK, slot * PAIRS + (h + 1) * TOK)
            hi, lo = split(qbuf[j, :, h * HEAD_DIM:(h + 1) * HEAD_DIM] * scale)
            for i, part in enumerate((hi, lo, hi, lo)):
                qcat[rows, i * 128:(i + 1) * 128] = part

    def prepare_k(zz):
        hi, lo = split(kvbuf[0, zz].reshape(TILE, HEAD_DIM))
        rows = pl.ds(pl.multiple_of(zz * TILE, TILE), TILE)
        for i, part in enumerate((hi, hi, lo, lo)):
            kcat[rows, i * 128:(i + 1) * 128] = part

    def prepare_v(zz):
        hi, lo = split(kvbuf[1, zz].reshape(TILE, HEAD_DIM))
        rows = pl.ds(pl.multiple_of(zz * TILE, TILE), TILE)
        vcat[rows, :128] = hi
        vcat[rows, 128:] = lo

    def scores(first, count, zz):
        keys = pl.ds(pl.multiple_of(zz * TILE, TILE), TILE)
        raw = lax.dot_general(
            qcat[first * PAIRS:(first + count) * PAIRS, :], kcat[keys, :], (((1,), (1,)), ((), ())),
            preferred_element_type=F32)
        for n in range(count):
            slot = first + n
            j = block_of(slot)
            rows = slice(slot * PAIRS, (slot + 1) * PAIRS)
            tokens = jnp.concatenate(
                [jnp.broadcast_to(cp[pl.ds(2 * j + i, 1), keys], (32, TILE)) for i in range(2)], axis=0)
            row = 256 * gr + 64 * j + lax.broadcasted_iota(jnp.int32, (TOK, TILE), 0)
            ok = (tokens <= row) & (tokens > jnp.concatenate([low[slot]] * (TILE // 128), axis=1))
            sc = raw[n * PAIRS:(n + 1) * PAIRS].reshape(HEADS, TOK, TILE)
            sc = jnp.where(ok[None], sc, NEG).reshape(PAIRS, TILE)
            s[rows, keys] = sc
            m = mx[rows, :]
            for a in range(TILE // 128):
                m = jnp.maximum(m, sc[:, a * 128:(a + 1) * 128])
            mx[rows, :] = m

    prepare_q(0)

    def warm(u, carry):
        advance(u)
        return carry

    lax.fori_loop(1 - AHEAD_A, 0, warm, 0)
    planes = z + 1

    for slot in (1, 2):
        q_arrival(DELTAS[slot]).wait_recv()
        prepare_q(slot)

    def near_step(u, carry):
        advance(u)
        c_arrival(0, z - u).wait_recv()
        prepare_k(z - u)
        scores(1, 2, z - u)
        return carry

    lax.fori_loop(0, planes, near_step, 0)

    q_arrival(DELTAS[3]).wait_recv()
    prepare_q(3)

    def slot_rows(slot):
        return pl.ds(pl.multiple_of(slot * PAIRS, PAIRS), PAIRS)

    def settle_max(slot, carry):
        rows = slot_rows(slot)
        m = jnp.maximum(jnp.max(mx[rows, :], axis=1, keepdims=True), FLOOR)
        mx[rows, :] = jnp.broadcast_to(m, (PAIRS, 128))
        return carry

    acc[...] = jnp.zeros_like(acc)
    lacc[...] = jnp.zeros_like(lacc)

    def weigh(slot, start, width):
        rows = slot_rows(slot)
        keys = pl.ds(pl.multiple_of(start * TILE, TILE), width)
        shift = jnp.concatenate([mx[rows, :]] * (width // 128), axis=1)
        p = jnp.exp2(s[rows, keys] - shift)
        hi, lo = split(p)
        v = vcat[keys, :]
        acc[rows, :] += jnp.dot(hi, v, preferred_element_type=F32) + jnp.dot(lo, v, preferred_element_type=F32)
        total = p[:, :128]
        for a in range(1, width // 128):
            total = total + p[:, a * 128:(a + 1) * 128]
        lacc[rows, :] += total

    def weigh_pair(slot, g):
        weigh(slot, z - 2 * g - 1, STEP)

    pairs = planes // 2

    early = ((3, 3, 0), (4, 3, 1), (5, 2, 0), (6, 3, 2), (7, 2, 1))

    def value_step(k, carry):
        advance(planes + k)
        for n in range(3):
            @pl.when(3 * k + n < planes)
            def _(n=n):
                scores(3, 1, z - 3 * k - n)

        @pl.when(k == jnp.minimum(z, 2))
        def _():
            lax.fori_loop(1, NX, settle_max, 0)
        @pl.when(k >= 3)
        def _():
            second = (k == 5) | (k == 7)
            weigh_pair(jnp.where(second, 2, 3), jnp.where(k == 6, 2, jnp.where((k == 4) | (k == 7), 1, 0)))
        c_arrival(1, z - k).wait_recv()
        prepare_v(z - k)
        return carry

    lax.fori_loop(0, planes, value_step, 0)

    def to_lanes(lse):
        spread = jnp.broadcast_to(lse, (PAIRS, 128)).reshape(HEADS, TOK, 128)
        return jnp.sum(jnp.where(eye[None], spread, 0.0), axis=1)

    def attend(slot, done):
        def pair_step(g, carry):
            weigh_pair(slot, g)
            return carry

        lax.fori_loop(done, pairs, pair_step, 0)

        @pl.when(planes % 2 == 1)
        def _():
            weigh(slot, 0, TILE)
        rows = slice(slot * PAIRS, (slot + 1) * PAIRS)
        total = jnp.sum(lacc[rows, :], axis=1, keepdims=True)
        some = total > 0
        inverse = jnp.where(some, 1.0 / jnp.where(some, total, 1.0), 0.0)
        lse = jnp.where(some, mx[rows, :] + jnp.log2(jnp.where(some, total, 1.0)), NEG)
        return (acc[rows, :128] + acc[rows, 128:]) * inverse, to_lanes(lse)

    for slot in (3, 2, 1):
        d = DELTAS[slot]
        done = jnp.int32(0)
        for k, of, _ in early:
            if of == slot:
                done += (planes > k).astype(jnp.int32)
        value, lse = attend(slot, done)
        lsend[d - 1] = lse
        l_copy(d).start()
        osend[d - 1] = value
        o_copy(d).start()

    def own_step(u, carry):
        scores(0, 1, z - u)
        return carry

    lax.fori_loop(0, planes, own_step, 0)
    settle_max(0, 0)
    value, lse = attend(0, 0)
    own[...] = value
    lsend[3] = lse

    for d in (1, 3, 2):
        l_copy(d).wait_recv()
    parts = [lsend[3], lrecv[0], lrecv[1], lrecv[2]]
    top = functools.reduce(jnp.maximum, parts)
    weights = [jnp.exp2(part - top) for part in parts]
    total = weights[0] + weights[1] + weights[2] + weights[3]
    ln_ref[...] = ((top + jnp.log2(total)) * math.log(2.0))[:, :TOK]
    shares = [weight / total for weight in weights]

    def column(share, h):
        return jnp.sum(jnp.where(eye, jnp.broadcast_to(share[h:h + 1, :], (TOK, 128)), 0.0), axis=1, keepdims=True)

    for h in range(HEADS):
        rows = slice(h * TOK, (h + 1) * TOK)
        out_ref[:, h * HEAD_DIM:(h + 1) * HEAD_DIM] = own[rows, :] * column(shares[0], h)
    for d in (2, 3, 1):
        o_copy(d).wait_recv()
        for h in range(HEADS):
            rows = slice(h * TOK, (h + 1) * TOK)
            out_ref[:, h * HEAD_DIM:(h + 1) * HEAD_DIM] += orecv[d - 1, rows, :] * column(shares[d], h)

    for d in (1, 2, 3):
        q_copy(d).wait_send()
        o_copy(d).wait_send()
        l_copy(d).wait_send()

    def drain_z(d, carry):
        @pl.when(straight(d))
        def _():
            z_copy(0, d).wait_send()
            z_copy(1, d).wait_send()
        return carry

    lax.fori_loop(1, NZ - z, drain_z, 0)

    for e in (1, 2):
        @pl.when((z >= 2) & (z + e < NZ - 1))
        def _(e=e):
            forward(0, e).wait_send()
            forward(1, e).wait_send()

    def drain(u, carry):
        w, zz = place(u)
        for d in (1, 2, 3):
            y_copy(w, zz, d).wait_send()
        c_copy(w, zz).wait_send()
        return carry

    lax.fori_loop(0, last + 1, drain, 0)


def shards(queries, keys, values, block_mask, key_lengths):
    lengths = key_lengths.reshape(128, 128)
    dma = pltpu.SemaphoreType.DMA
    anywhere = pl.BlockSpec(memory_space=pl.ANY)
    vmem = pl.BlockSpec(memory_space=pltpu.VMEM)
    return pl.pallas_call(
        kernel,
        out_shape=(
            jax.ShapeDtypeStruct((TOK, HEADS * HEAD_DIM), F32),
            jax.ShapeDtypeStruct((HEADS, TOK), F32),
        ),
        in_specs=[anywhere] * 5,
        out_specs=(vmem, vmem),
        scratch_shapes=[
            pltpu.VMEM((NX, TOK, HEADS * HEAD_DIM), F32),
            pltpu.VMEM((NX * PAIRS, 512), BF16),
            pltpu.VMEM((2, NZ, 2, NY, TOK, HEAD_DIM), F32),
            pltpu.VMEM((NZ * TILE, 512), BF16),
            pltpu.VMEM((NZ * TILE, 256), BF16),
            pltpu.VMEM((NX * PAIRS, NZ * TILE), F32),
            pltpu.VMEM((NX * PAIRS, 128), F32),
            pltpu.VMEM((NX * PAIRS, 256), F32),
            pltpu.VMEM((NX * PAIRS, 128), F32),
            pltpu.VMEM((3, PAIRS, 128), F32),
            pltpu.VMEM((4, HEADS, 128), F32),
            pltpu.VMEM((3, PAIRS, 128), F32),
            pltpu.VMEM((3, HEADS, 128), F32),
            pltpu.VMEM((PAIRS, 128), F32),
            pltpu.VMEM((8, 512), jnp.int32),
            pltpu.VMEM((8, 128), jnp.int32),
            pltpu.VMEM((NX, TOK, 128), jnp.int32),
            pltpu.VMEM((8, NZ * TILE), jnp.int32),
            dma((5,)),
            dma((NX,)), dma((NX,)),
            dma((2, NZ)), dma((2, NZ)), dma((2, 3)),
            dma((2, NZ, NY)), dma((2, NZ, NY)),
            dma((2, NZ)), dma((2, NZ)),
            dma((4,)), dma((4,)), dma((4,)), dma((4,)),
        ],
        compiler_params=pltpu.CompilerParams(
            vmem_limit_bytes=60 * 2**20, collective_id=0, has_side_effects=True),
        cost_estimate=pl.CostEstimate(flops=8 * 2 * 128 * 2**22, bytes_accessed=2**22, transcendentals=2**22),
    )(queries, keys, values, block_mask, lengths)


def solution(mesh):
    in_specs = (P(("qb", "kb"), None), P(("qb", "kb"), None), P(("qb", "kb"), None), P(), P())
    out_specs = (P(("qb", "kb"), None), P(None, ("qb", "kb")))
    return jax.shard_map(shards, mesh=mesh, in_specs=in_specs, out_specs=out_specs, check_vma=False)
```

```python
import functools
import math

import jax
import jax.numpy as jnp
from jax import lax
from jax.experimental import pallas as pl
from jax.experimental.pallas import tpu as pltpu
from jax.sharding import PartitionSpec as P

HEADS = 8
HEAD_DIM = 128
TOK = 64
PAIRS = HEADS * TOK
NX, NY, NZ = 4, 4, 8
TILE = 2 * NY * TOK
NEG = -1e30
FLOOR = -1e29
BIG = 1 << 30
MESH = pl.DeviceIdType.MESH
F32 = jnp.float32
BF16 = jnp.bfloat16
STEP = 2 * TILE
DELTAS = (0, 1, 3, 2)
AHEAD_A, AHEAD_C = 7, 2


def split(x):
    hi = x.astype(BF16)
    lo = (x - hi.astype(F32)).astype(BF16)
    return hi, lo


def kernel(
    q_ref, k_ref, v_ref, bm_ref, kl_ref, out_ref, ln_ref,
    qbuf, qcat, kvbuf, kcat, vcat, s, mx, acc, lacc, osend, lsend, orecv, lrecv, own, bm, lens, low, cp,
    local_sem, qs, qr, zs, zr, zf, ys, yr, cs, cr, os_, or_, ls_, lr_,
):
    qb = lax.axis_index("qb")
    kb = lax.axis_index("kb")
    z, c = lax.div(qb, 2), lax.rem(qb, 2)
    y, x = lax.div(kb, NX), lax.rem(kb, NX)
    gr = qb * NY + y
    last = 2 * z + 1
    partner = (qb + 1 - 2 * c, kb)

    def at_x(d):
        return (qb, y * NX + lax.rem(x + d, NX))

    def at_y(d):
        return (qb, lax.rem(y + d, NY) * NX + x)

    def at_z(d):
        return (lax.rem(qb + 2 * d, 2 * NZ), kb)

    loads = [
        pltpu.make_async_copy(k_ref, kvbuf.at[0, z, c, y], local_sem.at[0]),
        pltpu.make_async_copy(v_ref, kvbuf.at[1, z, c, y], local_sem.at[1]),
        pltpu.make_async_copy(q_ref, qbuf.at[x], local_sem.at[2]),
        pltpu.make_async_copy(bm_ref.at[pl.ds(pl.multiple_of(gr * 8, 8), 8)], bm, local_sem.at[3]),
        pltpu.make_async_copy(kl_ref.at[pl.ds(pl.multiple_of(qb * 8, 8), 8)], lens, local_sem.at[4]),
    ]
    for copy in loads:
        copy.start()

    barrier = pltpu.get_barrier_semaphore()
    peers = [at_x(d) for d in (1, 2, 3)] + [at_y(d) for d in (1, 2, 3)] + [partner]
    for peer in peers:
        pl.semaphore_signal(barrier, inc=1, device_id=peer, device_id_type=MESH)

    def greet(d, carry):
        pl.semaphore_signal(barrier, inc=1, device_id=at_z(NZ - d), device_id_type=MESH)
        return carry

    lax.fori_loop(1, z + 1, greet, 0)
    for copy in loads:
        copy.wait()
    pl.semaphore_wait(barrier, len(peers) + NZ - 1 - z)

    def remote(ref, send_sem, recv_sem, device, dst=None):
        return pltpu.make_async_remote_copy(
            src_ref=ref, dst_ref=ref if dst is None else dst, send_sem=send_sem, recv_sem=recv_sem,
            device_id=device, device_id_type=MESH)

    def q_copy(d):
        return remote(qbuf.at[x], qs.at[d], qr.at[x], at_x(d))

    def q_arrival(d):
        src = lax.rem(x + d, NX)
        return remote(qbuf.at[src], qs.at[0], qr.at[src], at_x(d))

    def z_copy(w, d):
        return remote(kvbuf.at[w, z, c, y], zs.at[w, d], zr.at[w, z], at_z(d))

    def straight(d):
        return (d < 3) | (d > 4) | (z + d == NZ - 1)

    def forward(w, e):
        return remote(kvbuf.at[w, z - 2, c, y], zf.at[w, e], zr.at[w, z - 2], at_z(e))

    def z_arrival(w, zz):
        return remote(kvbuf.at[w, zz, c, y], zs.at[w, 0], zr.at[w, zz], at_z(1))

    def y_copy(w, zz, d):
        return remote(kvbuf.at[w, zz, c, y], ys.at[w, zz, d], yr.at[w, zz, y], at_y(d))

    def y_arrival(w, zz, d):
        src = lax.rem(y + d, NY)
        return remote(kvbuf.at[w, zz, c, src], ys.at[w, zz, 0], yr.at[w, zz, src], at_y(d))

    def c_copy(w, zz):
        return remote(kvbuf.at[w, zz, c], cs.at[w, zz], cr.at[w, zz], partner)

    def c_arrival(w, zz):
        return remote(kvbuf.at[w, zz, 1 - c], cs.at[w, zz], cr.at[w, zz], partner)

    def o_copy(d):
        return remote(osend.at[d - 1], os_.at[d], or_.at[d], at_x(d), orecv.at[d - 1])

    def l_copy(d):
        return remote(lsend.at[d - 1], ls_.at[d], lr_.at[d], at_x(d), lrecv.at[d - 1])

    def place(u):
        w = (u > z).astype(jnp.int32)
        return w, z - u + w * (z + 1)

    def stage_a(u):
        w, zz = place(u)

        @pl.when(zz != z)
        def _():
            z_arrival(w, zz).wait_recv()
        for e in (1, 2):
            @pl.when((zz == z - 2) & (z + e < NZ - 1))
            def _(e=e):
                forward(w, e).start()
        for d in (2, 1, 3):
            y_copy(w, zz, d).start()

    def stage_c(u):
        w, zz = place(u)
        for d in (1, 3, 2):
            y_arrival(w, zz, d).wait_recv()
        c_copy(w, zz).start()

    def advance(u):
        for stage, ahead in ((stage_c, AHEAD_C), (stage_a, AHEAD_A)):
            step = u + ahead

            @pl.when((step >= 0) & (step <= last))
            def _(stage=stage, step=step):
                stage(step)

    stage_a(0)
    for d in (1, 3):
        q_copy(d).start()

    def send_z(w):
        def step(d, carry):
            @pl.when(straight(d))
            def _():
                z_copy(w, d).start()
            return carry
        lax.fori_loop(1, NZ - z, step, 0)

    send_z(0)
    q_copy(2).start()
    send_z(1)

    lane = lax.broadcasted_iota(jnp.int32, (8, 128), 1)
    sub = lax.broadcasted_iota(jnp.int32, (8, 128), 0)
    pick = 8 * (lane // 64) + 2 * x + (lane // 32) % 2
    for n in range(NZ * TILE // 128):
        bits = bm[:, (n // 8) * 128:(n // 8 + 1) * 128]
        here = jnp.take_along_axis(bits, pick + 16 * (n % 8), axis=1)
        column = 16 * n + pick
        token = 256 * (2 * n + lane // 64) + 64 * x + lane % 64
        cp[:, n * 128:(n + 1) * 128] = jnp.where((here == 1) | (column == 8 * gr + sub), token, BIG)

    scale = math.log2(math.e) / math.sqrt(HEAD_DIM)
    lane64 = lax.broadcasted_iota(jnp.int32, (TOK, 128), 1)
    sub64 = lax.broadcasted_iota(jnp.int32, (TOK, 128), 0)
    eye = lane64 == sub64

    def block_of(slot):
        return lax.rem(x + DELTAS[slot], NX)

    for slot in range(NX):
        j = block_of(slot)
        length_row = lens[pl.ds(2 * y + j // 2, 1), :]
        length = jnp.max(
            jnp.where(lane64 == sub64 + 64 * (j % 2), jnp.broadcast_to(length_row, (TOK, 128)), 0), axis=1, keepdims=True)
        low[slot] = 256 * gr + 64 * j + sub64 - length

    mx[...] = jnp.full(mx.shape, NEG, F32)

    def prepare_q(slot):
        j = block_of(slot)
        for h in range(HEADS):
            rows = slice(slot * PAIRS + h * TOK, slot * PAIRS + (h + 1) * TOK)
            hi, lo = split(qbuf[j, :, h * HEAD_DIM:(h + 1) * HEAD_DIM] * scale)
            for i, part in enumerate((hi, lo, hi, lo)):
                qcat[rows, i * 128:(i + 1) * 128] = part

    def prepare_k(zz):
        hi, lo = split(kvbuf[0, zz].reshape(TILE, HEAD_DIM))
        rows = pl.ds(pl.multiple_of(zz * TILE, TILE), TILE)
        for i, part in enumerate((hi, hi, lo, lo)):
            kcat[rows, i * 128:(i + 1) * 128] = part

    def prepare_v(zz):
        hi, lo = split(kvbuf[1, zz].reshape(TILE, HEAD_DIM))
        rows = pl.ds(pl.multiple_of(zz * TILE, TILE), TILE)
        vcat[rows, :128] = hi
        vcat[rows, 128:] = lo

    def scores(first, count, zz):
        keys = pl.ds(pl.multiple_of(zz * TILE, TILE), TILE)
        raw = lax.dot_general(
            qcat[first * PAIRS:(first + count) * PAIRS, :], kcat[keys, :], (((1,), (1,)), ((), ())),
            preferred_element_type=F32)
        for n in range(count):
            slot = first + n
            j = block_of(slot)
            rows = slice(slot * PAIRS, (slot + 1) * PAIRS)
            tokens = jnp.concatenate(
                [jnp.broadcast_to(cp[pl.ds(2 * j + i, 1), keys], (32, TILE)) for i in range(2)], axis=0)
            row = 256 * gr + 64 * j + lax.broadcasted_iota(jnp.int32, (TOK, TILE), 0)
            ok = (tokens <= row) & (tokens > jnp.concatenate([low[slot]] * (TILE // 128), axis=1))
            sc = raw[n * PAIRS:(n + 1) * PAIRS].reshape(HEADS, TOK, TILE)
            sc = jnp.where(ok[None], sc, NEG).reshape(PAIRS, TILE)
            s[rows, keys] = sc
            m = mx[rows, :]
            for a in range(TILE // 128):
                m = jnp.maximum(m, sc[:, a * 128:(a + 1) * 128])
            mx[rows, :] = m

    prepare_q(0)

    def warm(u, carry):
        advance(u)
        return carry

    lax.fori_loop(1 - AHEAD_A, 0, warm, 0)
    planes = z + 1

    for slot in (1, 2):
        q_arrival(DELTAS[slot]).wait_recv()
        prepare_q(slot)

    def near_step(u, carry):
        advance(u)
        c_arrival(0, z - u).wait_recv()
        prepare_k(z - u)
        scores(1, 2, z - u)
        return carry

    lax.fori_loop(0, planes, near_step, 0)

    q_arrival(DELTAS[3]).wait_recv()
    prepare_q(3)

    def slot_rows(slot):
        return pl.ds(pl.multiple_of(slot * PAIRS, PAIRS), PAIRS)

    def settle_max(slot, carry):
        rows = slot_rows(slot)
        m = jnp.maximum(jnp.max(mx[rows, :], axis=1, keepdims=True), FLOOR)
        mx[rows, :] = jnp.broadcast_to(m, (PAIRS, 128))
        return carry

    acc[...] = jnp.zeros_like(acc)
    lacc[...] = jnp.zeros_like(lacc)

    def weigh(slot, start, width):
        rows = slot_rows(slot)
        keys = pl.ds(pl.multiple_of(start * TILE, TILE), width)
        shift = jnp.concatenate([mx[rows, :]] * (width // 128), axis=1)
        p = jnp.exp2(s[rows, keys] - shift)
        hi, lo = split(p)
        v = vcat[keys, :]
        acc[rows, :] += jnp.dot(hi, v, preferred_element_type=F32) + jnp.dot(lo, v, preferred_element_type=F32)
        total = p[:, :128]
        for a in range(1, width // 128):
            total = total + p[:, a * 128:(a + 1) * 128]
        lacc[rows, :] += total

    def weigh_pair(slot, g):
        weigh(slot, z - 2 * g - 1, STEP)

    pairs = planes // 2

    early = ((3, 3, 0), (4, 3, 1), (5, 2, 0), (6, 3, 2), (7, 2, 1))

    def value_step(k, carry):
        advance(planes + k)
        for n in range(3):
            @pl.when(3 * k + n < planes)
            def _(n=n):
                scores(3, 1, z - 3 * k - n)

        @pl.when(k == jnp.minimum(z, 2))
        def _():
            lax.fori_loop(1, NX, settle_max, 0)
        @pl.when(k >= 3)
        def _():
            second = (k == 5) | (k == 7)
            weigh_pair(jnp.where(second, 2, 3), jnp.where(k == 6, 2, jnp.where((k == 4) | (k == 7), 1, 0)))
        c_arrival(1, z - k).wait_recv()
        prepare_v(z - k)
        return carry

    lax.fori_loop(0, planes, value_step, 0)

    def to_lanes(lse):
        spread = jnp.broadcast_to(lse, (PAIRS, 128)).reshape(HEADS, TOK, 128)
        return jnp.sum(jnp.where(eye[None], spread, 0.0), axis=1)

    def attend(slot, done):
        def pair_step(g, carry):
            weigh_pair(slot, g)
            return carry

        lax.fori_loop(done, pairs, pair_step, 0)

        @pl.when(planes % 2 == 1)
        def _():
            weigh(slot, 0, TILE)
        rows = slice(slot * PAIRS, (slot + 1) * PAIRS)
        total = jnp.sum(lacc[rows, :], axis=1, keepdims=True)
        some = total > 0
        inverse = jnp.where(some, 1.0 / jnp.where(some, total, 1.0), 0.0)
        lse = jnp.where(some, mx[rows, :] + jnp.log2(jnp.where(some, total, 1.0)), NEG)
        return (acc[rows, :128] + acc[rows, 128:]) * inverse, to_lanes(lse)

    for slot in (3, 2, 1):
        d = DELTAS[slot]
        done = jnp.int32(0)
        for k, of, _ in early:
            if of == slot:
                done += (planes > k).astype(jnp.int32)
        value, lse = attend(slot, done)
        lsend[d - 1] = lse
        l_copy(d).start()
        osend[d - 1] = value
        o_copy(d).start()

    def own_step(u, carry):
        scores(0, 1, z - u)
        return carry

    lax.fori_loop(0, planes, own_step, 0)
    settle_max(0, 0)
    value, lse = attend(0, 0)
    own[...] = value
    lsend[3] = lse

    for d in (1, 3, 2):
        l_copy(d).wait_recv()
    parts = [lsend[3], lrecv[0], lrecv[1], lrecv[2]]
    top = functools.reduce(jnp.maximum, parts)
    weights = [jnp.exp2(part - top) for part in parts]
    total = weights[0] + weights[1] + weights[2] + weights[3]
    ln_ref[...] = ((top + jnp.log2(total)) * math.log(2.0))[:, :TOK]
    shares = [weight / total for weight in weights]

    def column(share, h):
        return jnp.sum(jnp.where(eye, jnp.broadcast_to(share[h:h + 1, :], (TOK, 128)), 0.0), axis=1, keepdims=True)

    for h in range(HEADS):
        rows = slice(h * TOK, (h + 1) * TOK)
        out_ref[:, h * HEAD_DIM:(h + 1) * HEAD_DIM] = own[rows, :] * column(shares[0], h)
    for d in (2, 3, 1):
        o_copy(d).wait_recv()
        for h in range(HEADS):
            rows = slice(h * TOK, (h + 1) * TOK)
            out_ref[:, h * HEAD_DIM:(h + 1) * HEAD_DIM] += orecv[d - 1, rows, :] * column(shares[d], h)

    for d in (1, 2, 3):
        q_copy(d).wait_send()
        o_copy(d).wait_send()
        l_copy(d).wait_send()

    def drain_z(d, carry):
        @pl.when(straight(d))
        def _():
            z_copy(0, d).wait_send()
            z_copy(1, d).wait_send()
        return carry

    lax.fori_loop(1, NZ - z, drain_z, 0)

    for e in (1, 2):
        @pl.when((z >= 2) & (z + e < NZ - 1))
        def _(e=e):
            forward(0, e).wait_send()
            forward(1, e).wait_send()

    def drain(u, carry):
        w, zz = place(u)
        for d in (1, 2, 3):
            y_copy(w, zz, d).wait_send()
        c_copy(w, zz).wait_send()
        return carry

    lax.fori_loop(0, last + 1, drain, 0)


def shards(queries, keys, values, block_mask, key_lengths):
    lengths = key_lengths.reshape(128, 128)
    dma = pltpu.SemaphoreType.DMA
    anywhere = pl.BlockSpec(memory_space=pl.ANY)
    vmem = pl.BlockSpec(memory_space=pltpu.VMEM)
    return pl.pallas_call(
        kernel,
        out_shape=(
            jax.ShapeDtypeStruct((TOK, HEADS * HEAD_DIM), F32),
            jax.ShapeDtypeStruct((HEADS, TOK), F32),
        ),
        in_specs=[anywhere] * 5,
        out_specs=(vmem, vmem),
        scratch_shapes=[
            pltpu.VMEM((NX, TOK, HEADS * HEAD_DIM), F32),
            pltpu.VMEM((NX * PAIRS, 512), BF16),
            pltpu.VMEM((2, NZ, 2, NY, TOK, HEAD_DIM), F32),
            pltpu.VMEM((NZ * TILE, 512), BF16),
            pltpu.VMEM((NZ * TILE, 256), BF16),
            pltpu.VMEM((NX * PAIRS, NZ * TILE), F32),
            pltpu.VMEM((NX * PAIRS, 128), F32),
            pltpu.VMEM((NX * PAIRS, 256), F32),
            pltpu.VMEM((NX * PAIRS, 128), F32),
            pltpu.VMEM((3, PAIRS, 128), F32),
            pltpu.VMEM((4, HEADS, 128), F32),
            pltpu.VMEM((3, PAIRS, 128), F32),
            pltpu.VMEM((3, HEADS, 128), F32),
            pltpu.VMEM((PAIRS, 128), F32),
            pltpu.VMEM((8, 512), jnp.int32),
            pltpu.VMEM((8, 128), jnp.int32),
            pltpu.VMEM((NX, TOK, 128), jnp.int32),
            pltpu.VMEM((8, NZ * TILE), jnp.int32),
            dma((5,)),
            dma((NX,)), dma((NX,)),
            dma((2, NZ)), dma((2, NZ)), dma((2, 3)),
            dma((2, NZ, NY)), dma((2, NZ, NY)),
            dma((2, NZ)), dma((2, NZ)),
            dma((4,)), dma((4,)), dma((4,)), dma((4,)),
        ],
        compiler_params=pltpu.CompilerParams(
            vmem_limit_bytes=60 * 2**20, collective_id=0, has_side_effects=True),
        cost_estimate=pl.CostEstimate(flops=8 * 2 * 128 * 2**22, bytes_accessed=2**22, transcendentals=2**22),
    )(queries, keys, values, block_mask, lengths)


def solution(mesh):
    in_specs = (P(("qb", "kb"), None), P(("qb", "kb"), None), P(("qb", "kb"), None), P(), P())
    out_specs = (P(("qb", "kb"), None), P(None, ("qb", "kb")))
    return jax.shard_map(shards, mesh=mesh, in_specs=in_specs, out_specs=out_specs, check_vma=False)
```
